256 devices in a mesh: group: 64 (over x, y, z_lo), seq: 4 (over z_hi, core).
Axes of the slice: x: 4, y: 4, z: 8 (z_hi: 2, z_lo: 4; z = z_hi * 4 + z_lo), core: 2. Of those that a mesh axis runs over, the one named last changes fastest.
Arguments:
- queries: bfloat16 [32768, 6144], P(('group', 'seq')), may hold values from -32 to 32
- keys: bfloat16 [32768, 6144], P(('group', 'seq')), may hold values from -32 to 32
- values: bfloat16 [32768, 6144], P(('group', 'seq')), may hold values from -6 to 6
- noise_level: int32 [64], replicated, may hold values from 0 to 7
- block_mask: int32 [64, 3], replicated, may hold values 0 or 1
- gate_table: float32 [8, 6144], replicated, may hold values from 0.5 to 2
Outputs:
- gated: bfloat16 [32768, 6144], P(('group', 'seq'))
The draws below stay inside these ranges and needn't reach their ends.
All inputs are finite; a program needn't handle non-finite values.
Results may differ from the reference program's by a relative error of at most 0.008.
Values may be sent and summed in bfloat16 or wider, within the bound.
A program may use at most 128 MiB of HBM per device.

```python
import jax
import jax.numpy as jnp
from jax import lax

D = 6144
HEADS = 48
HD = 128
WINDOW = 3
LEVELS = 8
GROUPS = 64
CTOK = 512
TOKENS = 32768


def draw_queries(key, part):
    key = jax.random.fold_in(key, 1)
    result = jax.random.normal(key, (TOKENS, D), jnp.float32)
    return result.astype(jnp.bfloat16)


def draw_keys(key, part):
    key = jax.random.fold_in(key, 2)
    result = jax.random.normal(key, (TOKENS, D), jnp.float32)
    return result.astype(jnp.bfloat16)


def set_ends(values, stream_key, low, top_value):
    longest = values.shape.index(max(values.shape))
    spots = []
    for shift in (0, 1):
        where = [jax.random.randint(jax.random.fold_in(stream_key, axis), (), 0, length) for axis, length in enumerate(values.shape)]
        where[longest] = (where[longest] + shift) % values.shape[longest]
        spots.append(tuple(where))
    return values.at[spots[0]].set(low).at[spots[1]].set(top_value)


def shard_levels(own_key, shape, shards, smallest, top_value):
    level, own = 1.0, jax.random.fold_in(own_key, 6)
    for dim, blocks in shards:
        draws = jnp.exp(jax.random.uniform(jax.random.fold_in(own, dim), (blocks,), jnp.float32, smallest / len(shards), top_value / len(shards)))
        level = level * jnp.repeat(draws, shape[dim] // blocks).reshape([-1 if axis == dim else 1 for axis in range(len(shape))])
    return level


def gaussian(own_key, dims, width, bound, split=(), dtype=jnp.bfloat16):
    gain = shard_levels(own_key, dims, split, -0.22, 0.18) if split else 1.0
    values = jax.random.normal(own_key, dims, jnp.float32) * width * gain
    return jnp.minimum(jnp.maximum(values, -bound), bound).astype(dtype)


def setup_inputs(seed: int = 0) -> dict:
    seeds = jax.random.split(jax.random.key(seed), 7)
    queries = draw_queries(jax.random.fold_in(seeds[6], 71), 0)
    keys = draw_keys(jax.random.fold_in(seeds[6], 71), 0)
    values = gaussian(seeds[2], (TOKENS, D), 1.0, 6.0, ((0, 256),))
    noise_level = set_ends(jax.random.randint(seeds[3], (GROUPS,), 0, LEVELS), jax.random.fold_in(seeds[3], 1), 0, LEVELS - 1).astype(jnp.int32)
    block_mask = set_ends((jax.random.randint(seeds[4], (GROUPS, WINDOW), 0, 4) < 3).astype(jnp.int32), jax.random.fold_in(seeds[4], 1), 0, 1)
    gate_table = jnp.clip(jax.random.uniform(seeds[5], (LEVELS, D), jnp.float32, 0.5, 2.0), 0.5, 2.0)
    return dict(queries=queries, keys=keys, values=values, noise_level=noise_level, block_mask=block_mask, gate_table=gate_table)


def reference(queries, keys, values, noise_level, block_mask, gate_table):
    query_groups = queries.reshape(GROUPS, CTOK, HEADS, HD)
    padding = jnp.zeros((WINDOW, CTOK, HEADS, HD), jnp.bfloat16)
    keys_padded = jnp.concatenate([padding, keys.reshape(GROUPS, CTOK, HEADS, HD)], 0)
    values_padded = jnp.concatenate([padding, values.reshape(GROUPS, CTOK, HEADS, HD)], 0)
    offsets = (WINDOW - jnp.arange(WINDOW + 1)).astype(jnp.int32)
    scale = HD ** -0.5

    def attend_group(inputs):
        query_block, group_index = inputs
        key_window = lax.dynamic_slice_in_dim(keys_padded, group_index, WINDOW + 1, 0).reshape((WINDOW + 1) * CTOK, HEADS, HD)
        value_window = lax.dynamic_slice_in_dim(values_padded, group_index, WINDOW + 1, 0).reshape((WINDOW + 1) * CTOK, HEADS, HD)
        mask_row = lax.dynamic_index_in_dim(block_mask, group_index, 0, keepdims=False)
        allowed = jnp.concatenate([mask_row[::-1], jnp.ones((1,), jnp.int32)])
        visible = (allowed == 1) & (group_index - offsets >= 0)
        visible_keys = jnp.repeat(visible, CTOK)
        scores = jnp.einsum("qhd,khd->hqk", query_block.astype(jnp.float32), key_window.astype(jnp.float32)) * scale
        scores = jnp.where(visible_keys[None, None, :], scores, jnp.float32(-1e30))
        rowmax = jnp.max(scores, axis=-1, keepdims=True)
        weights = jnp.exp(scores - rowmax)
        total = jnp.sum(weights, axis=-1)
        weight_bf = lax.optimization_barrier(weights.astype(jnp.bfloat16))
        summed = jnp.einsum("hqk,khd->qhd", weight_bf.astype(jnp.float32), value_window.astype(jnp.float32))
        attended = summed / jnp.transpose(total)[:, :, None]
        return attended.reshape(CTOK, D).astype(jnp.bfloat16)

    attended = lax.map(attend_group, (query_groups, jnp.arange(GROUPS).astype(jnp.int32)))
    gate_rows = gate_table[noise_level]
    gated = attended.astype(jnp.float32) * gate_rows[:, None, :]
    return gated.astype(jnp.bfloat16).reshape(TOKENS, D)
```

```python
import functools

import jax
import jax.numpy as jnp
from jax import lax
from jax.experimental import pallas as pl
from jax.experimental.pallas import tpu as pltpu
from jax.sharding import PartitionSpec as P

HD = 128
WINDOW = 3
LEVELS = 8
ZLO = 4
SEQ = 4
RING = ZLO * SEQ
CTOK = 512
TOK = CTOK // SEQ
HEADS = 3
WIDTH = HEADS * HD
QROWS = 256
MESH = pl.DeviceIdType.MESH
PEERS = [(0, 1)] + [(r, b) for r in (1, 7, 2, 6, 3, 5, 4) for b in (0, 1)]


def block(i, size=HD):
    return pl.ds(pl.multiple_of(i * size, size), size)


def kernel(rings, q_ref, k_ref, v_ref, noise_ref, mask_ref, gate_ref, out_ref,
           qbuf, kbuf, vbuf, obuf, send, q_sem, k_sem, v_sem, halo_send, kh_sem, vh_sem, o_send, o_sem):
    group, seq = lax.axis_index("group"), lax.axis_index("seq")
    ring, zlo = group // ZLO, lax.rem(group, ZLO)
    core = lax.rem(seq, 2)
    z = (seq // 2) * ZLO + zlo

    def peer(r, b):
        z_there = lax.rem(z + r, 2 * ZLO)
        return lax.rem(z_there, ZLO), (z_there // ZLO) * 2 + lax.rem(core + b, 2)

    def device(place):
        return ring * ZLO + place[0], place[1]

    def heads_at(place):
        return (place[0] * SEQ + place[1]) * HEADS

    onward = lax.rem(ring + 1, rings) * ZLO + zlo, seq
    backward = lax.rem(ring + rings - 1, rings) * ZLO + zlo, seq

    barrier = pltpu.get_barrier_semaphore()
    for there in [device(peer(r, b)) for r, b in PEERS] + [onward, backward]:
        pl.semaphore_signal(barrier, inc=1, device_id=there, device_id_type=MESH)
    pl.semaphore_wait(barrier, len(PEERS) + 2)

    mine = heads_at((zlo, seq))
    place_q = zlo * SEQ + seq
    place_kv = place_q + WINDOW * SEQ

    def spread(src, buf, place, sem, send_sem, h):
        for r, b in PEERS:
            there = peer(r, b)
            pltpu.make_async_remote_copy(
                src_ref=src.at[:, block(heads_at(there) + h)],
                dst_ref=buf.at[h, block(place)],
                send_sem=send_sem,
                recv_sem=sem.at[h],
                device_id=device(there),
                device_id_type=MESH,
            ).start()
        pltpu.make_async_copy(src.at[:, block(mine + h)], buf.at[h, block(place)], sem.at[h]).start()

    @pl.loop(0, HEADS)
    def _(h):
        spread(k_ref, kbuf, place_kv, k_sem, send.at[0], h)
        spread(v_ref, vbuf, place_kv, v_sem, send.at[1], h)

    @pl.loop(0, HEADS)
    def _(h):
        spread(q_ref, qbuf, place_q, q_sem, send.at[2], h)

    def wait_bytes(part, sem):
        pltpu.make_async_copy(part, part, sem).wait()

    def halo(buf, sem, send_sem, h):
        return pltpu.make_async_remote_copy(
            src_ref=buf.at[h, pl.ds(ZLO * CTOK, WINDOW * CTOK)],
            dst_ref=buf.at[h, pl.ds(0, WINDOW * CTOK)],
            send_sem=send_sem.at[h],
            recv_sem=sem.at[h],
            device_id=onward,
            device_id_type=MESH,
        )

    @pl.loop(0, HEADS)
    def _(h):
        for i, (buf, sem, h_sem) in enumerate(((kbuf, k_sem, kh_sem), (vbuf, v_sem, vh_sem))):
            wait_bytes(buf.at[h, pl.ds(WINDOW * CTOK, ZLO * CTOK)], sem.at[h])
            halo(buf, h_sem, halo_send.at[i], h).start()

    factor = HD ** (-0.5) * 1.4426950408889634

    @pl.loop(0, HEADS)
    def _(h):
        wait_bytes(qbuf.at[h], q_sem.at[h])
        halo(kbuf, kh_sem, halo_send.at[0], h).wait_recv()
        halo(vbuf, vh_sem, halo_send.at[1], h).wait_recv()

        @pl.loop(0, ZLO)
        def _(step):
            g = lax.rem(zlo + step, ZLO)
            c = ring * ZLO + g
            seen = [
                (c - k >= 0) & (mask_ref[c, k - 1] == 1) if k else None for k in range(WINDOW, -1, -1)
            ]
            level = noise_ref[c]
            table = gate_ref[:, block(mine + h)]
            pick = lax.broadcasted_iota(jnp.int32, (LEVELS, HD), 0) == level
            gate = jnp.sum(jnp.where(pick, table, 0.0), axis=0, keepdims=True)

            @pl.loop(0, CTOK // QROWS)
            def _(part):
                rows = block(g * (CTOK // QROWS) + part, QROWS)
                q = qbuf[h, rows, :]
                scores, top = [], None
                for k in range(WINDOW + 1):
                    s = lax.dot_general(
                        q, kbuf[h, block(g + k, CTOK), :], (((1,), (1,)), ((), ())),
                        preferred_element_type=jnp.float32,
                    )
                    high = jnp.max(s, axis=1, keepdims=True)
                    if seen[k] is not None:
                        high = jnp.where(seen[k], high, -1e30)
                    top = high if top is None else jnp.maximum(top, high)
                    scores.append(s)
                top = top * factor
                total, summed = None, None
                for k in range(WINDOW + 1):
                    base = top if seen[k] is None else jnp.where(seen[k], top, 1e30)
                    weight = jnp.exp2(scores[k] * factor - base)
                    t = jnp.sum(weight, axis=1, keepdims=True)
                    o = jnp.dot(
                        weight.astype(jnp.bfloat16), vbuf[h, block(g + k, CTOK), :],
                        preferred_element_type=jnp.float32,
                    )
                    total = t if total is None else total + t
                    summed = o if summed is None else summed + o
                attended = (summed / total).astype(jnp.bfloat16)
                obuf[h, rows, :] = (attended.astype(jnp.float32) * gate).astype(jnp.bfloat16)

            for t in range(SEQ):
                s_there = lax.rem(seq + t, SEQ)
                src = obuf.at[h, block(g * SEQ + s_there)]
                dst = out_ref.at[:, block(mine + h)]

                def away():
                    pltpu.make_async_remote_copy(
                        src_ref=src, dst_ref=dst, send_sem=o_send, recv_sem=o_sem,
                        device_id=(c, s_there), device_id_type=MESH,
                    ).start()

                def here():
                    pltpu.make_async_copy(src, dst, o_sem).start()

                if t:
                    away()
                else:
                    pl.when(step == 0)(here)
                    pl.when(step != 0)(away)

    sent = pl.ds(0, (RING - 1) * TOK)
    wait_bytes(kbuf.at[:, sent], send.at[0])
    wait_bytes(vbuf.at[:, sent], send.at[1])
    wait_bytes(qbuf.at[:, sent], send.at[2])

    @pl.loop(0, HEADS)
    def _(h):
        halo(kbuf, kh_sem, halo_send.at[0], h).wait_send()
        halo(vbuf, vh_sem, halo_send.at[1], h).wait_send()

    wait_bytes(obuf.at[:, sent], o_send)
    wait_bytes(out_ref, o_sem)


def shards(rings, queries, keys, values, noise_level, block_mask, gate_table):
    anywhere = pl.BlockSpec(memory_space=pl.ANY)
    scalars = pl.BlockSpec(memory_space=pltpu.SMEM)
    dma = pltpu.SemaphoreType.DMA
    return pl.pallas_call(
        functools.partial(kernel, rings),
        out_shape=jax.ShapeDtypeStruct(queries.shape, queries.dtype),
        in_specs=[anywhere, anywhere, anywhere, scalars, scalars, pl.BlockSpec(memory_space=pltpu.VMEM)],
        out_specs=anywhere,
        scratch_shapes=[
            pltpu.VMEM((HEADS, ZLO * CTOK, HD), jnp.bfloat16),
            pltpu.VMEM((HEADS, (ZLO + WINDOW) * CTOK, HD), jnp.bfloat16),
            pltpu.VMEM((HEADS, (ZLO + WINDOW) * CTOK, HD), jnp.bfloat16),
            pltpu.VMEM((HEADS, ZLO * CTOK, HD), jnp.bfloat16),
            dma((3,)), dma((HEADS,)), dma((HEADS,)), dma((HEADS,)),
            dma((2, HEADS)), dma((HEADS,)), dma((HEADS,)), dma, dma,
        ],
        compiler_params=pltpu.CompilerParams(
            collective_id=0, has_side_effects=True, vmem_limit_bytes=48 * 2**20
        ),
    )(queries, keys, values, noise_level, block_mask, gate_table)


def solution(mesh):
    placed = (
        P(("group", "seq"), None),
        P(("group", "seq"), None),
        P(("group", "seq"), None),
        P(),
        P(),
        P(),
    )
    return jax.shard_map(
        functools.partial(shards, mesh.shape["group"] // ZLO),
        mesh=mesh, in_specs=placed, out_specs=P(("group", "seq"), None), check_vma=False,
    )
```

```python
import functools

import jax
import jax.numpy as jnp
from jax import lax
from jax.experimental import pallas as pl
from jax.experimental.pallas import tpu as pltpu
from jax.sharding import PartitionSpec as P

HD = 128
WINDOW = 3
LEVELS = 8
ZLO = 4
SEQ = 4
RING = ZLO * SEQ
CTOK = 512
TOK = CTOK // SEQ
HEADS = 3
WIDTH = HEADS * HD
QROWS = 256
MESH = pl.DeviceIdType.MESH
PEERS = [(r, b) for r in (4, 3, 5, 2, 6, 1, 7) for b in (0, 1)] + [(0, 1)]


def block(i, size=HD):
    return pl.ds(pl.multiple_of(i * size, size), size)


def kernel(rings, q_ref, k_ref, v_ref, noise_any, mask_any, gate_any, out_ref,
           noise_ref, mask_ref, gate_ref, small_sem, qbuf, kbuf, vbuf, obuf, send, q_sem, k_sem, v_sem, halo_send, kh_sem, vh_sem, o_send, o_sem):
    group, seq = lax.axis_index("group"), lax.axis_index("seq")
    ring, zlo = group // ZLO, lax.rem(group, ZLO)
    core = lax.rem(seq, 2)
    z = (seq // 2) * ZLO + zlo

    def peer(r, b):
        z_there = lax.rem(z + r, 2 * ZLO)
        return lax.rem(z_there, ZLO), (z_there // ZLO) * 2 + lax.rem(core + b, 2)

    def device(place):
        return ring * ZLO + place[0], place[1]

    def heads_at(place):
        return (place[0] * SEQ + place[1]) * HEADS

    onward = lax.rem(ring + 1, rings) * ZLO + zlo, seq
    backward = lax.rem(ring + rings - 1, rings) * ZLO + zlo, seq

    barrier = pltpu.get_barrier_semaphore()
    for there in [device(peer(r, b)) for r, b in PEERS] + [onward, backward]:
        pl.semaphore_signal(barrier, inc=1, device_id=there, device_id_type=MESH)
    mine = heads_at((zlo, seq))
    small = [
        pltpu.make_async_copy(noise_any, noise_ref, small_sem.at[0]),
        pltpu.make_async_copy(mask_any, mask_ref, small_sem.at[1]),
        pltpu.make_async_copy(gate_any.at[:, block(mine // HEADS, WIDTH)], gate_ref, small_sem.at[2]),
    ]
    for copy in small:
        copy.start()
    place_q = zlo * SEQ + seq
    place_kv = place_q + WINDOW * SEQ

    @pl.loop(0, HEADS)
    def _(h):
        for src, buf, place, sem in ((k_ref, kbuf, place_kv, k_sem), (v_ref, vbuf, place_kv, v_sem), (q_ref, qbuf, place_q, q_sem)):
            pltpu.make_async_copy(src.at[:, block(mine + h)], buf.at[h, block(place)], sem.at[h]).start()

    pl.semaphore_wait(barrier, len(PEERS) + 2)


    def spread(src, buf, place, sem, send_sem, h):
        for r, b in PEERS:
            there = peer(r, b)
            pltpu.make_async_remote_copy(
                src_ref=src.at[:, block(heads_at(there) + h)],
                dst_ref=buf.at[h, block(place)],
                send_sem=send_sem,
                recv_sem=sem.at[h],
                device_id=device(there),
                device_id_type=MESH,
            ).start()

    @pl.loop(0, HEADS)
    def _(h):
        spread(k_ref, kbuf, place_kv, k_sem, send.at[0], h)
        spread(v_ref, vbuf, place_kv, v_sem, send.at[1], h)

    @pl.loop(0, HEADS)
    def _(h):
        spread(q_ref, qbuf, place_q, q_sem, send.at[2], h)

    def wait_bytes(part, sem):
        pltpu.make_async_copy(part, part, sem).wait()

    def halo(buf, sem, send_sem, h):
        return pltpu.make_async_remote_copy(
            src_ref=buf.at[h, pl.ds(ZLO * CTOK, WINDOW * CTOK)],
            dst_ref=buf.at[h, pl.ds(0, WINDOW * CTOK)],
            send_sem=send_sem.at[h],
            recv_sem=sem.at[h],
            device_id=onward,
            device_id_type=MESH,
        )

    @pl.loop(0, HEADS)
    def _(h):
        for i, (buf, sem, h_sem) in enumerate(((kbuf, k_sem, kh_sem), (vbuf, v_sem, vh_sem))):
            wait_bytes(buf.at[h, pl.ds(WINDOW * CTOK, ZLO * CTOK)], sem.at[h])
            halo(buf, h_sem, halo_send.at[i], h).start()

    for copy in small:
        copy.wait()
    factor = HD ** (-0.5) * 1.4426950408889634

    @pl.loop(0, HEADS)
    def _(h):
        wait_bytes(qbuf.at[h], q_sem.at[h])
        halo(kbuf, kh_sem, halo_send.at[0], h).wait_recv()
        halo(vbuf, vh_sem, halo_send.at[1], h).wait_recv()

        @pl.loop(0, ZLO)
        def _(step):
            turn = lax.rem(2 * step + 1 - step // 2, ZLO)
            g = lax.rem(zlo + turn, ZLO)
            c = ring * ZLO + g
            seen = [
                (c - k >= 0) & (mask_ref[k - 1, c] == 1) if k else None for k in range(WINDOW, -1, -1)
            ]
            level = noise_ref[c]
            table = gate_ref[:, block(h)]
            pick = lax.broadcasted_iota(jnp.int32, (LEVELS, HD), 0) == level
            gate = jnp.sum(jnp.where(pick, table, 0.0), axis=0, keepdims=True)

            @pl.loop(0, CTOK // QROWS)
            def _(part):
                rows = block(g * (CTOK // QROWS) + part, QROWS)
                q = qbuf[h, rows, :]
                scores, top = [], None
                for k in range(WINDOW + 1):
                    s = lax.dot_general(
                        q, kbuf[h, block(g + k, CTOK), :], (((1,), (1,)), ((), ())),
                        preferred_element_type=jnp.float32,
                    )
                    high = jnp.max(s, axis=1, keepdims=True)
                    if seen[k] is not None:
                        high = jnp.where(seen[k], high, -1e30)
                    top = high if top is None else jnp.maximum(top, high)
                    scores.append(s)
                top = top * factor
                total, summed = None, None
                for k in range(WINDOW + 1):
                    base = top if seen[k] is None else jnp.where(seen[k], top, 1e30)
                    weight = jnp.exp2(scores[k] * factor - base)
                    t = jnp.sum(weight, axis=1, keepdims=True)
                    o = jnp.dot(
                        weight.astype(jnp.bfloat16), vbuf[h, block(g + k, CTOK), :],
                        preferred_element_type=jnp.float32,
                    )
                    total = t if total is None else total + t
                    summed = o if summed is None else summed + o
                attended = (summed / total).astype(jnp.bfloat16)
                obuf[h, rows, :] = (attended.astype(jnp.float32) * gate).astype(jnp.bfloat16)

            for t in range(SEQ):
                s_there = lax.rem(seq + t, SEQ)
                src = obuf.at[h, block(g * SEQ + s_there)]
                dst = out_ref.at[:, block(mine + h)]

                def away():
                    pltpu.make_async_remote_copy(
                        src_ref=src, dst_ref=dst, send_sem=o_send, recv_sem=o_sem,
                        device_id=(c, s_there), device_id_type=MESH,
                    ).start()

                def here():
                    pltpu.make_async_copy(src, dst, o_sem).start()

                if t:
                    away()
                else:
                    pl.when(turn == 0)(here)
                    pl.when(turn != 0)(away)

    sent = pl.ds(0, (RING - 1) * TOK)
    wait_bytes(kbuf.at[:, sent], send.at[0])
    wait_bytes(vbuf.at[:, sent], send.at[1])
    wait_bytes(qbuf.at[:, sent], send.at[2])

    @pl.loop(0, HEADS)
    def _(h):
        halo(kbuf, kh_sem, halo_send.at[0], h).wait_send()
        halo(vbuf, vh_sem, halo_send.at[1], h).wait_send()

    wait_bytes(obuf.at[:, sent], o_send)
    wait_bytes(out_ref, o_sem)


def shards(rings, queries, keys, values, noise_level, block_mask, gate_table):
    anywhere = pl.BlockSpec(memory_space=pl.ANY)
    dma = pltpu.SemaphoreType.DMA
    return pl.pallas_call(
        functools.partial(kernel, rings),
        out_shape=pltpu.VMEM(queries.shape, queries.dtype),
        in_specs=[anywhere] * 6,
        out_specs=anywhere,
        scratch_shapes=[
            pltpu.SMEM(noise_level.shape, jnp.int32),
            pltpu.SMEM(block_mask.shape[::-1], jnp.int32),
            pltpu.VMEM((LEVELS, WIDTH), jnp.float32),
            dma((3,)),
            pltpu.VMEM((HEADS, ZLO * CTOK, HD), jnp.bfloat16),
            pltpu.VMEM((HEADS, (ZLO + WINDOW) * CTOK, HD), jnp.bfloat16),
            pltpu.VMEM((HEADS, (ZLO + WINDOW) * CTOK, HD), jnp.bfloat16),
            pltpu.VMEM((HEADS, ZLO * CTOK, HD), jnp.bfloat16),
            dma((3,)), dma((HEADS,)), dma((HEADS,)), dma((HEADS,)),
            dma((2, HEADS)), dma((HEADS,)), dma((HEADS,)), dma, dma,
        ],
        compiler_params=pltpu.CompilerParams(
            collective_id=0, has_side_effects=True, vmem_limit_bytes=40 * 2**20
        ),
    )(*(pltpu.with_memory_space_constraint(x, pltpu.HBM) for x in (queries, keys, values, noise_level, block_mask.T, gate_table)))


def solution(mesh):
    placed = (
        P(("group", "seq"), None),
        P(("group", "seq"), None),
        P(("group", "seq"), None),
        P(),
        P(),
        P(),
    )
    return jax.shard_map(
        functools.partial(shards, mesh.shape["group"] // ZLO),
        mesh=mesh, in_specs=placed, out_specs=P(("group", "seq"), None), check_vma=False,
    )
```

```python
import functools

import jax
import jax.numpy as jnp
from jax import lax
from jax.experimental import pallas as pl
from jax.experimental.pallas import tpu as pltpu
from jax.sharding import PartitionSpec as P

HD = 128
WINDOW = 3
LEVELS = 8
ZLO = 4
SEQ = 4
RING = ZLO * SEQ
CTOK = 512
TOK = CTOK // SEQ
HEADS = 3
WIDTH = HEADS * HD
MESH = pl.DeviceIdType.MESH
PEERS = [(r, b) for r in (4, 3, 5, 2, 6, 1, 7) for b in (0, 1)] + [(0, 1)]


ORDER = (
    (1, 2, 3, 0),
    (0, 0, 0, 2),
    (3, 1, 1, 3),
    (5, 6, 7, 4),
    (2, 3, 2, 1),
    (6, 7, 4, 5),
    (7, 4, 5, 6),
    (4, 5, 6, 7),
)


def choose(i, options):
    result = options[-1]
    for j, option in enumerate(options[:-1]):
        result = jnp.where(i == j, option, result)
    return result


def block(i, size=HD):
    return pl.ds(pl.multiple_of(i * size, size), size)


def kernel(rings, q_ref, k_ref, v_ref, noise_any, mask_any, gate_any, out_ref,
           noise_ref, mask_ref, gate_ref, small_sem, qbuf, kbuf, vbuf, obuf, send, q_sem, k_sem, v_sem, go_sem, halo_send, kh_sem, vh_sem, o_send, o_sem):
    group, seq = lax.axis_index("group"), lax.axis_index("seq")
    ring, zlo = group // ZLO, lax.rem(group, ZLO)
    core = lax.rem(seq, 2)
    z = (seq // 2) * ZLO + zlo

    def peer(r, b):
        z_there = lax.rem(z + r, 2 * ZLO)
        return lax.rem(z_there, ZLO), (z_there // ZLO) * 2 + lax.rem(core + b, 2)

    def device(place):
        return ring * ZLO + place[0], place[1]

    def heads_at(place):
        return (place[0] * SEQ + place[1]) * HEADS

    hands_on, is_handed = ring < rings - 1, ring > 0
    onward = jnp.minimum(ring + 1, rings - 1) * ZLO + zlo, seq
    backward = jnp.maximum(ring - 1, 0) * ZLO + zlo, seq

    barrier = pltpu.get_barrier_semaphore()

    @pl.when(hands_on)
    def _():
        pl.semaphore_signal(barrier, inc=1, device_id=onward, device_id_type=MESH)

    for r, b in PEERS:
        pl.semaphore_signal(barrier, inc=1, device_id=device(peer(r, b)), device_id_type=MESH)
    mine = heads_at((zlo, seq))
    small = [
        pltpu.make_async_copy(noise_any, noise_ref, small_sem.at[0]),
        pltpu.make_async_copy(mask_any, mask_ref, small_sem.at[1]),
        pltpu.make_async_copy(gate_any.at[:, block(mine // HEADS, WIDTH)], gate_ref, small_sem.at[2]),
    ]
    for copy in small:
        copy.start()
    place_q = zlo * SEQ + seq
    place_kv = place_q + WINDOW * SEQ

    @pl.loop(0, HEADS)
    def _(h):
        for src, buf, place, sem in ((k_ref, kbuf, place_kv, k_sem), (v_ref, vbuf, place_kv, v_sem), (q_ref, qbuf, place_q, q_sem)):
            pltpu.make_async_copy(src.at[:, block(mine + h)], buf.at[h, block(place)], sem.at[h]).start()

    pl.semaphore_wait(barrier, len(PEERS) + is_handed.astype(jnp.int32))


    def spread(src, buf, place, sem, send_sem, h):
        for r, b in PEERS:
            there = peer(r, b)
            pltpu.make_async_remote_copy(
                src_ref=src.at[:, block(heads_at(there) + h)],
                dst_ref=buf.at[h, block(place)],
                send_sem=send_sem,
                recv_sem=sem.at[h],
                device_id=device(there),
                device_id_type=MESH,
            ).start()

    @pl.loop(0, HEADS)
    def _(h):
        spread(k_ref, kbuf, place_kv, k_sem, send.at[0], h)
        spread(v_ref, vbuf, place_kv, v_sem, send.at[1], h)

    @pl.loop(0, HEADS)
    def _(h):
        spread(q_ref, qbuf, place_q, q_sem, send.at[2], h)

    @pl.when(is_handed)
    def _():
        pl.semaphore_signal(go_sem, inc=1, device_id=backward, device_id_type=MESH)

    @pl.when(jnp.logical_not(is_handed))
    def _():
        nothing = jnp.zeros((HEADS, WINDOW * CTOK, HD), jnp.bfloat16)
        kbuf[:, pl.ds(0, WINDOW * CTOK), :] = nothing
        vbuf[:, pl.ds(0, WINDOW * CTOK), :] = nothing

    @pl.when(hands_on)
    def _():
        pl.semaphore_wait(go_sem, 1)

    def wait_bytes(part, sem):
        pltpu.make_async_copy(part, part, sem).wait()

    def halo(buf, sem, send_sem, h):
        return pltpu.make_async_remote_copy(
            src_ref=buf.at[h, pl.ds(ZLO * CTOK, WINDOW * CTOK)],
            dst_ref=buf.at[h, pl.ds(0, WINDOW * CTOK)],
            send_sem=send_sem.at[h],
            recv_sem=sem.at[h],
            device_id=onward,
            device_id_type=MESH,
        )

    @pl.loop(0, HEADS)
    def _(h):
        for i, (buf, sem, h_sem) in enumerate(((kbuf, k_sem, kh_sem), (vbuf, v_sem, vh_sem))):
            wait_bytes(buf.at[h, pl.ds(WINDOW * CTOK, ZLO * CTOK)], sem.at[h])
            pl.when(hands_on)(halo(buf, h_sem, halo_send.at[i], h).start)

    for copy in small:
        copy.wait()
    factor = HD ** (-0.5) * 1.4426950408889634

    @pl.loop(0, HEADS)
    def _(h):
        wait_bytes(qbuf.at[h], q_sem.at[h])
        pl.when(is_handed)(halo(kbuf, kh_sem, halo_send.at[0], h).wait_recv)
        pl.when(is_handed)(halo(vbuf, vh_sem, halo_send.at[1], h).wait_recv)

        @pl.loop(0, 2 * ZLO)
        def _(step):
            z_there = choose(step, [choose(zlo, column) for column in ORDER])
            g, half = lax.rem(z_there, ZLO), z_there // ZLO
            c = ring * ZLO + g
            seen = [
                (c - k >= 0) & (mask_ref[k - 1, c] == 1) if k else None for k in range(WINDOW, -1, -1)
            ]
            level = noise_ref[c]
            table = gate_ref[:, block(h)]
            pick = lax.broadcasted_iota(jnp.int32, (LEVELS, HD), 0) == level
            gate = jnp.sum(jnp.where(pick, table, 0.0), axis=0, keepdims=True)

            rows = block(g * 2 + half, CTOK // 2)
            q = qbuf[h, rows, :]
            scores, top = [], None
            for k in range(WINDOW + 1):
                s = lax.dot_general(
                    q, kbuf[h, block(g + k, CTOK), :], (((1,), (1,)), ((), ())),
                    preferred_element_type=jnp.float32,
                )
                high = jnp.max(s, axis=1, keepdims=True)
                if seen[k] is not None:
                    high = jnp.where(seen[k], high, -1e30)
                top = high if top is None else jnp.maximum(top, high)
                scores.append(s)
            top = top * factor
            total, summed = None, None
            for k in range(WINDOW + 1):
                base = top if seen[k] is None else jnp.where(seen[k], top, 1e30)
                weight = jnp.exp2(scores[k] * factor - base)
                t = jnp.sum(weight, axis=1, keepdims=True)
                o = jnp.dot(
                    weight.astype(jnp.bfloat16), vbuf[h, block(g + k, CTOK), :],
                    preferred_element_type=jnp.float32,
                )
                total = t if total is None else total + t
                summed = o if summed is None else summed + o
            attended = (summed / total).astype(jnp.bfloat16)
            obuf[h, rows, :] = (attended.astype(jnp.float32) * gate).astype(jnp.bfloat16)

            for t in range(2):
                s_there = half * 2 + lax.rem(core + t, 2)
                src = obuf.at[h, block(g * SEQ + s_there)]
                dst = out_ref.at[:, block(mine + h)]

                def away():
                    pltpu.make_async_remote_copy(
                        src_ref=src, dst_ref=dst, send_sem=o_send, recv_sem=o_sem,
                        device_id=(c, s_there), device_id_type=MESH,
                    ).start()

                def here():
                    pltpu.make_async_copy(src, dst, o_sem).start()

                if t:
                    away()
                else:
                    pl.when(z_there == z)(here)
                    pl.when(z_there != z)(away)

    sent = pl.ds(0, (RING - 1) * TOK)
    wait_bytes(kbuf.at[:, sent], send.at[0])
    wait_bytes(vbuf.at[:, sent], send.at[1])
    wait_bytes(qbuf.at[:, sent], send.at[2])

    @pl.loop(0, HEADS)
    def _(h):
        pl.when(hands_on)(halo(kbuf, kh_sem, halo_send.at[0], h).wait_send)
        pl.when(hands_on)(halo(vbuf, vh_sem, halo_send.at[1], h).wait_send)

    wait_bytes(obuf.at[:, sent], o_send)
    wait_bytes(out_ref, o_sem)


def shards(rings, queries, keys, values, noise_level, block_mask, gate_table):
    anywhere = pl.BlockSpec(memory_space=pl.ANY)
    dma = pltpu.SemaphoreType.DMA
    return pl.pallas_call(
        functools.partial(kernel, rings),
        out_shape=pltpu.VMEM(queries.shape, queries.dtype),
        in_specs=[anywhere] * 6,
        out_specs=anywhere,
        scratch_shapes=[
            pltpu.SMEM(noise_level.shape, jnp.int32),
            pltpu.SMEM(block_mask.shape[::-1], jnp.int32),
            pltpu.VMEM((LEVELS, WIDTH), jnp.float32),
            dma((3,)),
            pltpu.VMEM((HEADS, ZLO * CTOK, HD), jnp.bfloat16),
            pltpu.VMEM((HEADS, (ZLO + WINDOW) * CTOK, HD), jnp.bfloat16),
            pltpu.VMEM((HEADS, (ZLO + WINDOW) * CTOK, HD), jnp.bfloat16),
            pltpu.VMEM((HEADS, ZLO * CTOK, HD), jnp.bfloat16),
            dma((3,)), dma((HEADS,)), dma((HEADS,)), dma((HEADS,)),
            pltpu.SemaphoreType.REGULAR,
            dma((2, HEADS)), dma((HEADS,)), dma((HEADS,)), dma, dma,
        ],
        compiler_params=pltpu.CompilerParams(
            collective_id=0, has_side_effects=True, vmem_limit_bytes=40 * 2**20
        ),
    )(*(pltpu.with_memory_space_constraint(x, pltpu.HBM) for x in (queries, keys, values, noise_level, block_mask.T, gate_table)))


def solution(mesh):
    placed = (
        P(("group", "seq"), None),
        P(("group", "seq"), None),
        P(("group", "seq"), None),
        P(),
        P(),
        P(),
    )
    return jax.shard_map(
        functools.partial(shards, mesh.shape["group"] // ZLO),
        mesh=mesh, in_specs=placed, out_specs=P(("group", "seq"), None), check_vma=False,
    )
```

```python
import functools

import jax
import jax.numpy as jnp
from jax import lax
from jax.experimental import pallas as pl
from jax.experimental.pallas import tpu as pltpu
from jax.sharding import PartitionSpec as P

HD = 128
WINDOW = 3
LEVELS = 8
ZLO = 4
SEQ = 4
RING = ZLO * SEQ
ROW = 4
CTOK = 512
TOK = CTOK // SEQ
HEADS = 3
WIDTH = HEADS * HD
MESH = pl.DeviceIdType.MESH
PEERS = [(r, b) for r in (4, 3, 5, 2, 6, 1, 7) for b in (0, 1)] + [(0, 1)]


ORDER = (
    (1, 0, 0, 1),
    (2, 2, 1, 0),
    (0, 1, 2, 2),
    (5, 6, 7, 4),
    (3, 3, 3, 3),
    (6, 7, 4, 5),
    (7, 4, 5, 6),
    (4, 5, 6, 7),
)


def choose(i, options):
    result = options[-1]
    for j, option in enumerate(options[:-1]):
        result = jnp.where(i == j, option, result)
    return result


def block(i, size=HD):
    return pl.ds(pl.multiple_of(i * size, size), size)


def kernel(rings, q_ref, k_ref, v_ref, noise_any, mask_any, gate_any, out_ref,
           noise_ref, mask_ref, gate_ref, small_sem, qbuf, kbuf, vbuf, obuf, send, q_sem, k_sem, v_sem, go_sem, halo_send, kh_sem, vh_sem, o_send, o_sem):
    group, seq = lax.axis_index("group"), lax.axis_index("seq")
    ring, zlo = group // ZLO, lax.rem(group, ZLO)
    core = lax.rem(seq, 2)
    z = (seq // 2) * ZLO + zlo

    def peer(r, b):
        z_there = lax.rem(z + r, 2 * ZLO)
        return lax.rem(z_there, ZLO), (z_there // ZLO) * 2 + lax.rem(core + b, 2)

    def device(place):
        return ring * ZLO + place[0], place[1]

    def heads_at(place):
        return (place[0] * SEQ + place[1]) * HEADS

    hands_on, is_handed = ring < rings - 1, ring > 0
    starts_row, ends_row = lax.rem(ring, ROW) == 0, lax.rem(ring, ROW) == ROW - 1
    waits_behind, leaves_behind = is_handed & jnp.logical_not(starts_row), is_handed & starts_row
    waits_ahead, leaves_ahead = hands_on & ends_row, hands_on & jnp.logical_not(ends_row)
    onward = jnp.minimum(ring + 1, rings - 1) * ZLO + zlo, seq
    backward = jnp.maximum(ring - 1, 0) * ZLO + zlo, seq

    barrier = pltpu.get_barrier_semaphore()

    @pl.when(leaves_ahead)
    def _():
        pl.semaphore_signal(barrier, inc=1, device_id=onward, device_id_type=MESH)

    @pl.when(leaves_behind)
    def _():
        pl.semaphore_signal(barrier, inc=1, device_id=backward, device_id_type=MESH)

    for r, b in PEERS:
        pl.semaphore_signal(barrier, inc=1, device_id=device(peer(r, b)), device_id_type=MESH)
    mine = heads_at((zlo, seq))
    small = [
        pltpu.make_async_copy(noise_any, noise_ref, small_sem.at[0]),
        pltpu.make_async_copy(mask_any, mask_ref, small_sem.at[1]),
        pltpu.make_async_copy(gate_any.at[:, block(mine // HEADS, WIDTH)], gate_ref, small_sem.at[2]),
    ]
    for copy in small:
        copy.start()
    place_q = zlo * SEQ + seq
    place_kv = place_q + WINDOW * SEQ

    @pl.loop(0, HEADS)
    def _(h):
        for src, buf, place, sem in ((k_ref, kbuf, place_kv, k_sem), (v_ref, vbuf, place_kv, v_sem), (q_ref, qbuf, place_q, q_sem)):
            pltpu.make_async_copy(src.at[:, block(mine + h)], buf.at[h, block(place)], sem.at[h]).start()

    pl.semaphore_wait(barrier, len(PEERS) + waits_behind.astype(jnp.int32) + waits_ahead.astype(jnp.int32))


    def spread(src, buf, place, sem, send_sem, h):
        for r, b in PEERS:
            there = peer(r, b)
            pltpu.make_async_remote_copy(
                src_ref=src.at[:, block(heads_at(there) + h)],
                dst_ref=buf.at[h, block(place)],
                send_sem=send_sem,
                recv_sem=sem.at[h],
                device_id=device(there),
                device_id_type=MESH,
            ).start()

    @pl.loop(0, HEADS)
    def _(h):
        spread(k_ref, kbuf, place_kv, k_sem, send.at[0], h)
        spread(v_ref, vbuf, place_kv, v_sem, send.at[1], h)

    @pl.loop(0, HEADS)
    def _(h):
        spread(q_ref, qbuf, place_q, q_sem, send.at[2], h)

    @pl.when(waits_behind)
    def _():
        pl.semaphore_signal(go_sem, inc=1, device_id=backward, device_id_type=MESH)

    @pl.when(jnp.logical_not(is_handed))
    def _():
        nothing = jnp.zeros((HEADS, WINDOW * CTOK, HD), jnp.bfloat16)
        kbuf[:, pl.ds(0, WINDOW * CTOK), :] = nothing
        vbuf[:, pl.ds(0, WINDOW * CTOK), :] = nothing

    @pl.when(leaves_ahead)
    def _():
        pl.semaphore_wait(go_sem, 1)

    def wait_bytes(part, sem):
        pltpu.make_async_copy(part, part, sem).wait()

    def halo(buf, sem, send_sem, h):
        return pltpu.make_async_remote_copy(
            src_ref=buf.at[h, pl.ds(ZLO * CTOK, WINDOW * CTOK)],
            dst_ref=buf.at[h, pl.ds(0, WINDOW * CTOK)],
            send_sem=send_sem.at[h],
            recv_sem=sem.at[h],
            device_id=onward,
            device_id_type=MESH,
        )

    @pl.loop(0, HEADS)
    def _(h):
        for i, (buf, sem, h_sem) in enumerate(((kbuf, k_sem, kh_sem), (vbuf, v_sem, vh_sem))):
            wait_bytes(buf.at[h, pl.ds(WINDOW * CTOK, ZLO * CTOK)], sem.at[h])
            pl.when(hands_on)(halo(buf, h_sem, halo_send.at[i], h).start)

    for copy in small:
        copy.wait()
    factor = HD ** (-0.5) * 1.4426950408889634

    @pl.loop(0, HEADS)
    def _(h):
        wait_bytes(qbuf.at[h], q_sem.at[h])
        pl.when(is_handed)(halo(kbuf, kh_sem, halo_send.at[0], h).wait_recv)
        pl.when(is_handed)(halo(vbuf, vh_sem, halo_send.at[1], h).wait_recv)

        @pl.loop(0, 2 * ZLO)
        def _(step):
            z_there = choose(step, [choose(zlo, column) for column in ORDER])
            g, half = lax.rem(z_there, ZLO), z_there // ZLO
            c = ring * ZLO + g
            seen = [
                (c - k >= 0) & (mask_ref[k - 1, c] == 1) if k else None for k in range(WINDOW, -1, -1)
            ]
            level = noise_ref[c]
            table = gate_ref[:, block(h)]
            pick = lax.broadcasted_iota(jnp.int32, (LEVELS, HD), 0) == level
            gate = jnp.sum(jnp.where(pick, table, 0.0), axis=0, keepdims=True)

            rows = block(g * 2 + half, CTOK // 2)
            q = qbuf[h, rows, :]
            scores, top = [], None
            for k in range(WINDOW + 1):
                s = lax.dot_general(
                    q, kbuf[h, block(g + k, CTOK), :], (((1,), (1,)), ((), ())),
                    preferred_element_type=jnp.float32,
                )
                high = jnp.max(s, axis=1, keepdims=True)
                if seen[k] is not None:
                    high = jnp.where(seen[k], high, -1e30)
                top = high if top is None else jnp.maximum(top, high)
                scores.append(s)
            top = top * factor
            total, summed = None, None
            for k in range(WINDOW + 1):
                base = top if seen[k] is None else jnp.where(seen[k], top, 1e30)
                weight = jnp.exp2(scores[k] * factor - base)
                t = jnp.sum(weight, axis=1, keepdims=True)
                o = jnp.dot(
                    weight.astype(jnp.bfloat16), vbuf[h, block(g + k, CTOK), :],
                    preferred_element_type=jnp.float32,
                )
                total = t if total is None else total + t
                summed = o if summed is None else summed + o
            attended = (summed / total).astype(jnp.bfloat16)
            obuf[h, rows, :] = (attended.astype(jnp.float32) * gate).astype(jnp.bfloat16)

            for t in range(2):
                s_there = half * 2 + lax.rem(core + t, 2)
                src = obuf.at[h, block(g * SEQ + s_there)]
                dst = out_ref.at[:, block(mine + h)]

                def away():
                    pltpu.make_async_remote_copy(
                        src_ref=src, dst_ref=dst, send_sem=o_send, recv_sem=o_sem,
                        device_id=(c, s_there), device_id_type=MESH,
                    ).start()

                def here():
                    pltpu.make_async_copy(src, dst, o_sem).start()

                if t:
                    away()
                else:
                    pl.when(z_there == z)(here)
                    pl.when(z_there != z)(away)

    sent = pl.ds(0, (RING - 1) * TOK)
    wait_bytes(kbuf.at[:, sent], send.at[0])
    wait_bytes(vbuf.at[:, sent], send.at[1])
    wait_bytes(qbuf.at[:, sent], send.at[2])

    @pl.loop(0, HEADS)
    def _(h):
        pl.when(hands_on)(halo(kbuf, kh_sem, halo_send.at[0], h).wait_send)
        pl.when(hands_on)(halo(vbuf, vh_sem, halo_send.at[1], h).wait_send)

    wait_bytes(obuf.at[:, sent], o_send)
    wait_bytes(out_ref, o_sem)


def shards(rings, queries, keys, values, noise_level, block_mask, gate_table):
    anywhere = pl.BlockSpec(memory_space=pl.ANY)
    dma = pltpu.SemaphoreType.DMA
    return pl.pallas_call(
        functools.partial(kernel, rings),
        out_shape=pltpu.VMEM(queries.shape, queries.dtype),
        in_specs=[anywhere] * 6,
        out_specs=anywhere,
        scratch_shapes=[
            pltpu.SMEM(noise_level.shape, jnp.int32),
            pltpu.SMEM(block_mask.shape[::-1], jnp.int32),
            pltpu.VMEM((LEVELS, WIDTH), jnp.float32),
            dma((3,)),
            pltpu.VMEM((HEADS, ZLO * CTOK, HD), jnp.bfloat16),
            pltpu.VMEM((HEADS, (ZLO + WINDOW) * CTOK, HD), jnp.bfloat16),
            pltpu.VMEM((HEADS, (ZLO + WINDOW) * CTOK, HD), jnp.bfloat16),
            pltpu.VMEM((HEADS, ZLO * CTOK, HD), jnp.bfloat16),
            dma((3,)), dma((HEADS,)), dma((HEADS,)), dma((HEADS,)),
            pltpu.SemaphoreType.REGULAR,
            dma((2, HEADS)), dma((HEADS,)), dma((HEADS,)), dma, dma,
        ],
        compiler_params=pltpu.CompilerParams(
            collective_id=0, has_side_effects=True, vmem_limit_bytes=40 * 2**20
        ),
    )(*(pltpu.with_memory_space_constraint(x, pltpu.HBM) for x in (queries, keys, values, noise_level, block_mask.T, gate_table)))


def solution(mesh):
    placed = (
        P(("group", "seq"), None),
        P(("group", "seq"), None),
        P(("group", "seq"), None),
        P(),
        P(),
        P(),
    )
    return jax.shard_map(
        functools.partial(shards, mesh.shape["group"] // ZLO),
        mesh=mesh, in_specs=placed, out_specs=P(("group", "seq"), None), check_vma=False,
    )
```

```python
import functools

import jax
import jax.numpy as jnp
from jax import lax
from jax.experimental import pallas as pl
from jax.experimental.pallas import tpu as pltpu
from jax.sharding import PartitionSpec as P

HD = 128
WINDOW = 3
LEVELS = 8
ZLO = 4
SEQ = 4
RING = ZLO * SEQ
ROW = 4
CTOK = 512
TOK = CTOK // SEQ
HEADS = 3
WIDTH = HEADS * HD
MESH = pl.DeviceIdType.MESH
PEERS = [(r, b) for r in (1, 7, 2, 6, 3, 5, 4) for b in (0, 1)] + [(0, 1)]


ORDER = (
    (1, 0, 0, 1),
    (2, 2, 1, 0),
    (0, 1, 2, 2),
    (5, 6, 7, 4),
    (3, 3, 3, 3),
    (6, 7, 4, 5),
    (7, 4, 5, 6),
    (4, 5, 6, 7),
)


def choose(i, options):
    result = options[-1]
    for j, option in enumerate(options[:-1]):
        result = jnp.where(i == j, option, result)
    return result


def block(i, size=HD):
    return pl.ds(pl.multiple_of(i * size, size), size)


def kernel(rings, q_ref, k_ref, v_ref, noise_any, mask_any, gate_any, out_ref,
           noise_ref, mask_ref, gate_ref, small_sem, qbuf, kbuf, vbuf, obuf, send, q_sem, k_sem, v_sem, go_sem, halo_send, kh_sem, vh_sem, o_send, o_sem):
    group, seq = lax.axis_index("group"), lax.axis_index("seq")
    ring, zlo = group // ZLO, lax.rem(group, ZLO)
    core = lax.rem(seq, 2)
    z = (seq // 2) * ZLO + zlo

    def peer(r, b):
        z_there = lax.rem(z + r, 2 * ZLO)
        return lax.rem(z_there, ZLO), (z_there // ZLO) * 2 + lax.rem(core + b, 2)

    def device(place):
        return ring * ZLO + place[0], place[1]

    def heads_at(place):
        return (place[0] * SEQ + place[1]) * HEADS

    hands_on, is_handed = ring < rings - 1, ring > 0
    starts_row, ends_row = lax.rem(ring, ROW) == 0, lax.rem(ring, ROW) == ROW - 1
    waits_behind, leaves_behind = is_handed & jnp.logical_not(starts_row), is_handed & starts_row
    waits_ahead, leaves_ahead = hands_on & ends_row, hands_on & jnp.logical_not(ends_row)
    onward = jnp.minimum(ring + 1, rings - 1) * ZLO + zlo, seq
    backward = jnp.maximum(ring - 1, 0) * ZLO + zlo, seq

    barrier = pltpu.get_barrier_semaphore()

    @pl.when(leaves_ahead)
    def _():
        pl.semaphore_signal(barrier, inc=1, device_id=onward, device_id_type=MESH)

    @pl.when(leaves_behind)
    def _():
        pl.semaphore_signal(barrier, inc=1, device_id=backward, device_id_type=MESH)

    for r, b in PEERS:
        pl.semaphore_signal(barrier, inc=1, device_id=device(peer(r, b)), device_id_type=MESH)
    mine = heads_at((zlo, seq))
    small = [
        pltpu.make_async_copy(noise_any, noise_ref, small_sem.at[0]),
        pltpu.make_async_copy(mask_any, mask_ref, small_sem.at[1]),
        pltpu.make_async_copy(gate_any.at[:, block(mine // HEADS, WIDTH)], gate_ref, small_sem.at[2]),
    ]
    for copy in small:
        copy.start()
    place_q = zlo * SEQ + seq
    place_kv = place_q + WINDOW * SEQ

    @pl.loop(0, HEADS)
    def _(h):
        for src, buf, place, sem in ((k_ref, kbuf, place_kv, k_sem), (v_ref, vbuf, place_kv, v_sem), (q_ref, qbuf, place_q, q_sem)):
            pltpu.make_async_copy(src.at[:, block(mine + h)], buf.at[h, block(place)], sem.at[h]).start()

    pl.semaphore_wait(barrier, len(PEERS) + waits_behind.astype(jnp.int32) + waits_ahead.astype(jnp.int32))


    def spread(src, buf, place, sem, send_sem, h):
        for r, b in PEERS:
            there = peer(r, b)
            pltpu.make_async_remote_copy(
                src_ref=src.at[:, block(heads_at(there) + h)],
                dst_ref=buf.at[h, block(place)],
                send_sem=send_sem,
                recv_sem=sem.at[h],
                device_id=device(there),
                device_id_type=MESH,
            ).start()

    @pl.loop(0, HEADS)
    def _(h):
        spread(k_ref, kbuf, place_kv, k_sem, send.at[0], h)
        spread(v_ref, vbuf, place_kv, v_sem, send.at[1], h)

    @pl.loop(0, HEADS)
    def _(h):
        spread(q_ref, qbuf, place_q, q_sem, send.at[2], h)

    @pl.when(waits_behind)
    def _():
        pl.semaphore_signal(go_sem, inc=1, device_id=backward, device_id_type=MESH)

    @pl.when(jnp.logical_not(is_handed))
    def _():
        nothing = jnp.zeros((HEADS, WINDOW * CTOK, HD), jnp.bfloat16)
        kbuf[:, pl.ds(0, WINDOW * CTOK), :] = nothing
        vbuf[:, pl.ds(0, WINDOW * CTOK), :] = nothing

    @pl.when(leaves_ahead)
    def _():
        pl.semaphore_wait(go_sem, 1)

    def wait_bytes(part, sem):
        pltpu.make_async_copy(part, part, sem).wait()

    def halo(buf, sem, send_sem, h):
        return pltpu.make_async_remote_copy(
            src_ref=buf.at[h, pl.ds(ZLO * CTOK, WINDOW * CTOK)],
            dst_ref=buf.at[h, pl.ds(0, WINDOW * CTOK)],
            send_sem=send_sem.at[h],
            recv_sem=sem.at[h],
            device_id=onward,
            device_id_type=MESH,
        )

    @pl.loop(0, HEADS)
    def _(h):
        for i, (buf, sem, h_sem) in enumerate(((kbuf, k_sem, kh_sem), (vbuf, v_sem, vh_sem))):
            wait_bytes(buf.at[h, pl.ds(WINDOW * CTOK, ZLO * CTOK)], sem.at[h])
            pl.when(hands_on)(halo(buf, h_sem, halo_send.at[i], h).start)

    for copy in small:
        copy.wait()
    factor = HD ** (-0.5) * 1.4426950408889634

    @pl.loop(0, HEADS)
    def _(h):
        wait_bytes(qbuf.at[h], q_sem.at[h])
        pl.when(is_handed)(halo(kbuf, kh_sem, halo_send.at[0], h).wait_recv)
        pl.when(is_handed)(halo(vbuf, vh_sem, halo_send.at[1], h).wait_recv)

        @pl.loop(0, 2 * ZLO)
        def _(step):
            z_there = choose(step, [choose(zlo, column) for column in ORDER])
            g, half = lax.rem(z_there, ZLO), z_there // ZLO
            c = ring * ZLO + g
            seen = [
                (c - k >= 0) & (mask_ref[k - 1, c] == 1) if k else None for k in range(WINDOW, -1, -1)
            ]
            level = noise_ref[c]
            table = gate_ref[:, block(h)]
            pick = lax.broadcasted_iota(jnp.int32, (LEVELS, HD), 0) == level
            gate = jnp.sum(jnp.where(pick, table, 0.0), axis=0, keepdims=True)

            rows = block(g * 2 + half, CTOK // 2)
            q = qbuf[h, rows, :]
            scores, top = [], None
            for k in range(WINDOW + 1):
                s = lax.dot_general(
                    q, kbuf[h, block(g + k, CTOK), :], (((1,), (1,)), ((), ())),
                    preferred_element_type=jnp.float32,
                )
                high = jnp.max(s, axis=1, keepdims=True)
                if seen[k] is not None:
                    high = jnp.where(seen[k], high, -1e30)
                top = high if top is None else jnp.maximum(top, high)
                scores.append(s)
            top = top * factor
            total, summed = None, None
            for k in range(WINDOW + 1):
                base = top if seen[k] is None else jnp.where(seen[k], top, 1e30)
                weight = jnp.exp2(scores[k] * factor - base)
                t = jnp.sum(weight, axis=1, keepdims=True)
                o = jnp.dot(
                    weight.astype(jnp.bfloat16), vbuf[h, block(g + k, CTOK), :],
                    preferred_element_type=jnp.float32,
                )
                total = t if total is None else total + t
                summed = o if summed is None else summed + o
            attended = (summed / total).astype(jnp.bfloat16)
            obuf[h, rows, :] = (attended.astype(jnp.float32) * gate).astype(jnp.bfloat16)

            for t in range(2):
                s_there = half * 2 + 1 - t
                src = obuf.at[h, block(g * SEQ + s_there)]
                dst = out_ref.at[:, block(mine + h)]

                def away():
                    pltpu.make_async_remote_copy(
                        src_ref=src, dst_ref=dst, send_sem=o_send, recv_sem=o_sem,
                        device_id=(c, s_there), device_id_type=MESH,
                    ).start()

                def here():
                    pltpu.make_async_copy(src, dst, o_sem).start()

                own = (z_there == z) & (core == 1 - t)
                pl.when(own)(here)
                pl.when(jnp.logical_not(own))(away)

    sent = pl.ds(0, (RING - 1) * TOK)
    wait_bytes(kbuf.at[:, sent], send.at[0])
    wait_bytes(vbuf.at[:, sent], send.at[1])
    wait_bytes(qbuf.at[:, sent], send.at[2])

    @pl.loop(0, HEADS)
    def _(h):
        pl.when(hands_on)(halo(kbuf, kh_sem, halo_send.at[0], h).wait_send)
        pl.when(hands_on)(halo(vbuf, vh_sem, halo_send.at[1], h).wait_send)

    wait_bytes(obuf.at[:, sent], o_send)
    wait_bytes(out_ref, o_sem)


def shards(rings, queries, keys, values, noise_level, block_mask, gate_table):
    anywhere = pl.BlockSpec(memory_space=pl.ANY)
    dma = pltpu.SemaphoreType.DMA
    return pl.pallas_call(
        functools.partial(kernel, rings),
        out_shape=pltpu.VMEM(queries.shape, queries.dtype),
        in_specs=[anywhere] * 6,
        out_specs=anywhere,
        scratch_shapes=[
            pltpu.SMEM(noise_level.shape, jnp.int32),
            pltpu.SMEM(block_mask.shape[::-1], jnp.int32),
            pltpu.VMEM((LEVELS, WIDTH), jnp.float32),
            dma((3,)),
            pltpu.VMEM((HEADS, ZLO * CTOK, HD), jnp.bfloat16),
            pltpu.VMEM((HEADS, (ZLO + WINDOW) * CTOK, HD), jnp.bfloat16),
            pltpu.VMEM((HEADS, (ZLO + WINDOW) * CTOK, HD), jnp.bfloat16),
            pltpu.VMEM((HEADS, ZLO * CTOK, HD), jnp.bfloat16),
            dma((3,)), dma((HEADS,)), dma((HEADS,)), dma((HEADS,)),
            pltpu.SemaphoreType.REGULAR,
            dma((2, HEADS)), dma((HEADS,)), dma((HEADS,)), dma, dma,
        ],
        compiler_params=pltpu.CompilerParams(
            collective_id=0, has_side_effects=True, vmem_limit_bytes=40 * 2**20
        ),
    )(*(pltpu.with_memory_space_constraint(x, pltpu.HBM) for x in (queries, keys, values, noise_level, block_mask.T, gate_table)))


def solution(mesh):
    placed = (
        P(("group", "seq"), None),
        P(("group", "seq"), None),
        P(("group", "seq"), None),
        P(),
        P(),
        P(),
    )
    return jax.shard_map(
        functools.partial(shards, mesh.shape["group"] // ZLO),
        mesh=mesh, in_specs=placed, out_specs=P(("group", "seq"), None), check_vma=False,
    )
```

```python
import functools

import jax
import jax.numpy as jnp
from jax import lax
from jax.experimental import pallas as pl
from jax.experimental.pallas import tpu as pltpu
from jax.sharding import PartitionSpec as P

HD = 128
WINDOW = 3
LEVELS = 8
ZLO = 4
SEQ = 4
RING = ZLO * SEQ
ROW = 4
CTOK = 512
TOK = CTOK // SEQ
HEADS = 3
WIDTH = HEADS * HD
MESH = pl.DeviceIdType.MESH
PEERS = [(r, b) for r in (1, 7, 2, 6, 3, 5, 4) for b in (0, 1)] + [(0, 1)]


ORDER = (
    (1, 0, 0, 1),
    (2, 2, 1, 0),
    (0, 1, 2, 2),
    (5, 6, 7, 4),
    (3, 3, 3, 3),
    (6, 7, 4, 5),
    (7, 4, 5, 6),
    (4, 5, 6, 7),
)


def choose(i, options):
    result = options[-1]
    for j, option in enumerate(options[:-1]):
        result = jnp.where(i == j, option, result)
    return result


def block(i, size=HD):
    return pl.ds(pl.multiple_of(i * size, size), size)


def kernel(rings, q_ref, k_ref, v_ref, noise_any, mask_any, gate_any, out_ref,
           noise_ref, mask_ref, gate_ref, small_sem, qbuf, kbuf, vbuf, obuf, send, q_sem, k_sem, v_sem, go_sem, halo_send, kh_sem, vh_sem, o_send, o_sem):
    group, seq = lax.axis_index("group"), lax.axis_index("seq")
    ring, zlo = group // ZLO, lax.rem(group, ZLO)
    core = lax.rem(seq, 2)
    z = (seq // 2) * ZLO + zlo

    def peer(r, b):
        z_there = lax.rem(z + r, 2 * ZLO)
        return lax.rem(z_there, ZLO), (z_there // ZLO) * 2 + lax.rem(core + b, 2)

    def device(place):
        return ring * ZLO + place[0], place[1]

    def heads_at(place):
        return (place[0] * SEQ + place[1]) * HEADS

    hands_on, is_handed = ring < rings - 1, ring > 0
    starts_row, ends_row = lax.rem(ring, ROW) == 0, lax.rem(ring, ROW) == ROW - 1
    waits_behind, leaves_behind = is_handed & jnp.logical_not(starts_row), is_handed & starts_row
    waits_ahead, leaves_ahead = hands_on & ends_row, hands_on & jnp.logical_not(ends_row)
    onward = jnp.minimum(ring + 1, rings - 1) * ZLO + zlo, seq
    backward = jnp.maximum(ring - 1, 0) * ZLO + zlo, seq

    barrier = pltpu.get_barrier_semaphore()

    for r, b in reversed(PEERS):
        pl.semaphore_signal(barrier, inc=1, device_id=device(peer(r, b)), device_id_type=MESH)

    @pl.when(leaves_ahead)
    def _():
        pl.semaphore_signal(barrier, inc=1, device_id=onward, device_id_type=MESH)

    @pl.when(leaves_behind)
    def _():
        pl.semaphore_signal(barrier, inc=1, device_id=backward, device_id_type=MESH)

    mine = heads_at((zlo, seq))
    small = [
        pltpu.make_async_copy(noise_any, noise_ref, small_sem.at[0]),
        pltpu.make_async_copy(mask_any, mask_ref, small_sem.at[1]),
        pltpu.make_async_copy(gate_any.at[:, block(mine // HEADS, WIDTH)], gate_ref, small_sem.at[2]),
    ]
    for copy in small:
        copy.start()
    place_q = zlo * SEQ + seq
    place_kv = place_q + WINDOW * SEQ

    @pl.loop(0, HEADS)
    def _(h):
        for src, buf, place, sem in ((k_ref, kbuf, place_kv, k_sem), (v_ref, vbuf, place_kv, v_sem), (q_ref, qbuf, place_q, q_sem)):
            pltpu.make_async_copy(src.at[:, block(mine + h)], buf.at[h, block(place)], sem.at[h]).start()

    pl.semaphore_wait(barrier, len(PEERS) + waits_behind.astype(jnp.int32) + waits_ahead.astype(jnp.int32))


    def spread(src, buf, place, sem, send_sem, h):
        for r, b in PEERS:
            there = peer(r, b)
            pltpu.make_async_remote_copy(
                src_ref=src.at[:, block(heads_at(there) + h)],
                dst_ref=buf.at[h, block(place)],
                send_sem=send_sem,
                recv_sem=sem.at[h],
                device_id=device(there),
                device_id_type=MESH,
            ).start()

    @pl.loop(0, HEADS)
    def _(h):
        spread(k_ref, kbuf, place_kv, k_sem, send.at[0], h)
        spread(v_ref, vbuf, place_kv, v_sem, send.at[1], h)

    @pl.loop(0, HEADS)
    def _(h):
        spread(q_ref, qbuf, place_q, q_sem, send.at[2], h)

    @pl.when(waits_behind)
    def _():
        pl.semaphore_signal(go_sem, inc=1, device_id=backward, device_id_type=MESH)

    @pl.when(jnp.logical_not(is_handed))
    def _():
        nothing = jnp.zeros((HEADS, WINDOW * CTOK, HD), jnp.bfloat16)
        kbuf[:, pl.ds(0, WINDOW * CTOK), :] = nothing
        vbuf[:, pl.ds(0, WINDOW * CTOK), :] = nothing

    @pl.when(leaves_ahead)
    def _():
        pl.semaphore_wait(go_sem, 1)

    def wait_bytes(part, sem):
        pltpu.make_async_copy(part, part, sem).wait()

    def halo(buf, sem, send_sem, h):
        return pltpu.make_async_remote_copy(
            src_ref=buf.at[h, pl.ds(ZLO * CTOK, WINDOW * CTOK)],
            dst_ref=buf.at[h, pl.ds(0, WINDOW * CTOK)],
            send_sem=send_sem.at[h],
            recv_sem=sem.at[h],
            device_id=onward,
            device_id_type=MESH,
        )

    @pl.loop(0, HEADS)
    def _(h):
        for i, (buf, sem, h_sem) in enumerate(((kbuf, k_sem, kh_sem), (vbuf, v_sem, vh_sem))):
            wait_bytes(buf.at[h, pl.ds(WINDOW * CTOK, ZLO * CTOK)], sem.at[h])
            pl.when(hands_on)(halo(buf, h_sem, halo_send.at[i], h).start)

    for copy in small:
        copy.wait()
    factor = HD ** (-0.5) * 1.4426950408889634

    @pl.loop(0, HEADS)
    def _(h):
        wait_bytes(qbuf.at[h], q_sem.at[h])
        pl.when(is_handed)(halo(kbuf, kh_sem, halo_send.at[0], h).wait_recv)
        pl.when(is_handed)(halo(vbuf, vh_sem, halo_send.at[1], h).wait_recv)

        @pl.loop(0, 2 * ZLO)
        def _(step):
            z_there = choose(step, [choose(zlo, column) for column in ORDER])
            g, half = lax.rem(z_there, ZLO), z_there // ZLO
            c = ring * ZLO + g
            seen = [
                (c - k >= 0) & (mask_ref[k - 1, c] == 1) if k else None for k in range(WINDOW, -1, -1)
            ]
            level = noise_ref[c]
            table = gate_ref[:, block(h)]
            pick = lax.broadcasted_iota(jnp.int32, (LEVELS, HD), 0) == level
            gate = jnp.sum(jnp.where(pick, table, 0.0), axis=0, keepdims=True)

            rows = block(g * 2 + half, CTOK // 2)
            q = qbuf[h, rows, :]
            scores, top = [], None
            for k in range(WINDOW + 1):
                s = lax.dot_general(
                    q, kbuf[h, block(g + k, CTOK), :], (((1,), (1,)), ((), ())),
                    preferred_element_type=jnp.float32,
                )
                high = jnp.max(s, axis=1, keepdims=True)
                if seen[k] is not None:
                    high = jnp.where(seen[k], high, -1e30)
                top = high if top is None else jnp.maximum(top, high)
                scores.append(s)
            top = top * factor
            total, summed = None, None
            for k in range(WINDOW + 1):
                base = top if seen[k] is None else jnp.where(seen[k], top, 1e30)
                weight = jnp.exp2(scores[k] * factor - base)
                t = jnp.sum(weight, axis=1, keepdims=True)
                o = jnp.dot(
                    weight.astype(jnp.bfloat16), vbuf[h, block(g + k, CTOK), :],
                    preferred_element_type=jnp.float32,
                )
                total = t if total is None else total + t
                summed = o if summed is None else summed + o
            attended = (summed / total).astype(jnp.bfloat16)
            obuf[h, rows, :] = (attended.astype(jnp.float32) * gate).astype(jnp.bfloat16)

            for t in range(2):
                s_there = half * 2 + 1 - t
                src = obuf.at[h, block(g * SEQ + s_there)]
                dst = out_ref.at[:, block(mine + h)]

                def away():
                    pltpu.make_async_remote_copy(
                        src_ref=src, dst_ref=dst, send_sem=o_send, recv_sem=o_sem,
                        device_id=(c, s_there), device_id_type=MESH,
                    ).start()

                def here():
                    pltpu.make_async_copy(src, dst, o_sem).start()

                own = (z_there == z) & (core == 1 - t)
                pl.when(own)(here)
                pl.when(jnp.logical_not(own))(away)

    sent = pl.ds(0, (RING - 1) * TOK)
    wait_bytes(kbuf.at[:, sent], send.at[0])
    wait_bytes(vbuf.at[:, sent], send.at[1])
    wait_bytes(qbuf.at[:, sent], send.at[2])

    @pl.loop(0, HEADS)
    def _(h):
        pl.when(hands_on)(halo(kbuf, kh_sem, halo_send.at[0], h).wait_send)
        pl.when(hands_on)(halo(vbuf, vh_sem, halo_send.at[1], h).wait_send)

    wait_bytes(obuf.at[:, sent], o_send)
    wait_bytes(out_ref, o_sem)


def shards(rings, queries, keys, values, noise_level, block_mask, gate_table):
    anywhere = pl.BlockSpec(memory_space=pl.ANY)
    dma = pltpu.SemaphoreType.DMA
    return pl.pallas_call(
        functools.partial(kernel, rings),
        out_shape=pltpu.VMEM(queries.shape, queries.dtype),
        in_specs=[anywhere] * 6,
        out_specs=anywhere,
        scratch_shapes=[
            pltpu.SMEM(noise_level.shape, jnp.int32),
            pltpu.SMEM(block_mask.shape[::-1], jnp.int32),
            pltpu.VMEM((LEVELS, WIDTH), jnp.float32),
            dma((3,)),
            pltpu.VMEM((HEADS, ZLO * CTOK, HD), jnp.bfloat16),
            pltpu.VMEM((HEADS, (ZLO + WINDOW) * CTOK, HD), jnp.bfloat16),
            pltpu.VMEM((HEADS, (ZLO + WINDOW) * CTOK, HD), jnp.bfloat16),
            pltpu.VMEM((HEADS, ZLO * CTOK, HD), jnp.bfloat16),
            dma((3,)), dma((HEADS,)), dma((HEADS,)), dma((HEADS,)),
            pltpu.SemaphoreType.REGULAR,
            dma((2, HEADS)), dma((HEADS,)), dma((HEADS,)), dma, dma,
        ],
        compiler_params=pltpu.CompilerParams(
            collective_id=0, has_side_effects=True, vmem_limit_bytes=40 * 2**20
        ),
    )(*(pltpu.with_memory_space_constraint(x, pltpu.HBM) for x in (queries, keys, values, noise_level, block_mask.T, gate_table)))


def solution(mesh):
    placed = (
        P(("group", "seq"), None),
        P(("group", "seq"), None),
        P(("group", "seq"), None),
        P(),
        P(),
        P(),
    )
    return jax.shard_map(
        functools.partial(shards, mesh.shape["group"] // ZLO),
        mesh=mesh, in_specs=placed, out_specs=P(("group", "seq"), None), check_vma=False,
    )
```
